32 devices in a mesh: dp: 4 (over y, x), pipe: 8 (over z, core).
Axes of the slice: x: 2, y: 2, z: 4, core: 2. Of those that a mesh axis runs over, the one named last changes fastest.
Arguments:
- weights: bfloat16 [8, 2, 3840, 512], P('pipe'), as said below
- master: float32 [8, 3840, 512], P('pipe', 'dp')
- moment1: bfloat16 [8, 3840, 512], P('pipe', 'dp'), may hold values from -1.5 to 1.5
- moment2: bfloat16 [8, 3840, 512], P('pipe', 'dp'), may hold values from 0.0099487305 to 1
- saved: bfloat16 [8, 2, 4, 64, 3840], P('pipe', None, None, 'dp')
- cotangent: bfloat16 [2, 4, 64, 3840], P(None, None, 'dp'), may hold values from -0.75 to 0.75
Outputs:
- new_master: float32 [8, 3840, 512], P('pipe', 'dp')
- new_moment1: bfloat16 [8, 3840, 512], P('pipe', 'dp')
- new_moment2: bfloat16 [8, 3840, 512], P('pipe', 'dp')
The draws below stay inside these ranges and needn't reach their ends.
Inputs may be any that keep to these rules, and one draw needn't show every extreme that they name: weights[i, 1] equals weights[7 - i, 0], and weights[i, 0] is master[i] rounded to bfloat16.
All inputs are finite; a program needn't handle non-finite values.
Results may differ from the reference program's by a relative error of at most 0.0075.
Values may be sent and summed in bfloat16 or wider, within the bound.
A program may use at most 128 MiB of HBM per device.

```python
import math
import jax
import jax.numpy as jnp
from jax import lax

D = 3840
RANK = 256
MICRO = 4
SECTIONS = 8
TOKENS = 64
N_DP = 4


def master_values(key):
    array_shape = (SECTIONS, D, 2 * RANK)
    normal_part = jax.random.normal(jax.random.fold_in(key, 11), array_shape, jnp.float32)
    values = normal_part
    columns = jnp.arange(2 * RANK)
    column_scale = jnp.where(columns < RANK, float(D) ** (-0.5), float(RANK * SECTIONS) ** (-0.5)).astype(jnp.float32)
    return values * column_scale


def draw_master(key, part):
    values = master_values(key)
    return values


def draw_weights(key, part):
    values = master_values(key).astype(jnp.bfloat16)
    return jnp.stack([values, values[::-1]], axis=1)


def draw_saved(key, part):
    key = jax.random.fold_in(key, 5)
    array_shape = (SECTIONS, 2, MICRO, TOKENS, D)
    values = jax.random.normal(jax.random.fold_in(key, 1), array_shape, jnp.float32)
    spread = math.log(10.0)
    row_scale = jnp.exp(jax.random.uniform(jax.random.fold_in(key, 2), (SECTIONS, 2, MICRO, TOKENS, 1), jnp.float32, 0.0, spread))
    column_scale = jnp.exp(jax.random.uniform(jax.random.fold_in(key, 3), (SECTIONS, 2, 1, 1, D), jnp.float32, 0.0, spread))
    return (values * row_scale * column_scale).astype(jnp.bfloat16)


def block_levels(rng, dims, shards, low, largest):
    def one(axis_at, blocks):
        heights = jax.random.uniform(jax.random.fold_in(jax.random.fold_in(rng, 6), axis_at), (blocks,), jnp.float32, low / len(shards), largest / len(shards))
        return jnp.repeat(jnp.exp(heights), dims[axis_at] // blocks).reshape((-1,) + (1,) * (len(dims) - axis_at - 1))

    level = one(*shards[0])
    for cut in shards[1:]:
        level = level * one(*cut)
    return level


def scatter_about(rng, dims, deviation, most, pieces=(), kind=jnp.bfloat16):
    gain = block_levels(rng, dims, pieces, -0.22, 0.18) if pieces else 1.0
    entries = jax.random.normal(rng, dims, jnp.float32) * deviation * gain
    return jnp.minimum(jnp.maximum(entries, -most), most).astype(kind)


def setup_inputs(seed: int = 0) -> dict:
    key_of = jax.random.split(jax.random.key(seed), 7)
    return {
        "weights": draw_weights(jax.random.fold_in(key_of[6], 71), 0),
        "master": draw_master(jax.random.fold_in(key_of[6], 71), 0),
        "moment1": scatter_about(key_of[2], (SECTIONS, D, 2 * RANK), 0.1, 1.5, ((0, 8), (1, 4))),
        "moment2": jnp.clip(jnp.exp(math.log(1.0) - 4.61031033 * jax.random.uniform(key_of[3], (SECTIONS, D, 2 * RANK), jnp.float32) ** block_levels(key_of[3], (SECTIONS, D, 2 * RANK), ((0, 8), (1, 4)), -0.2, 0.2)), 0.0099487305, 1.0).astype(jnp.bfloat16),
        "saved": draw_saved(jax.random.fold_in(key_of[6], 71), 0),
        "cotangent": scatter_about(key_of[5], (2, MICRO, TOKENS, D), 0.05, 0.75, ((2, 4),)),
    }


norm_epsilon = 1e-06
first_decay = 0.9
second_decay = 0.95
adam_epsilon = 1e-08
learn_rate = 0.00022
weight_decay = 0.1
step_count = 100.0

def section_backward(inputs, grad_out, section_weights):
    latent_width = section_weights.shape[1] // 2
    down_proj = section_weights[:, :latent_width]
    up_proj = section_weights[:, latent_width:]
    values = inputs.astype(jnp.float32)
    row_scale = lax.rsqrt(lax.optimization_barrier(jnp.mean(values * values, axis=-1, keepdims=True)) + norm_epsilon)
    normed = (values * row_scale).astype(jnp.bfloat16)
    latent = jnp.dot(normed, down_proj, preferred_element_type=jnp.float32)
    latent_scale = lax.rsqrt(lax.optimization_barrier(jnp.mean(latent * latent, axis=-1, keepdims=True)) + norm_epsilon)
    latent_act = (latent * latent_scale).astype(jnp.bfloat16)
    grad_act = jnp.dot(grad_out, up_proj, preferred_element_type=jnp.float32)
    grad_latent = latent_scale * grad_act - latent * latent_scale ** 3 * lax.optimization_barrier(jnp.mean(latent * grad_act, axis=-1, keepdims=True))
    grad_latent = grad_latent.astype(jnp.bfloat16)
    grad_normed = jnp.dot(grad_latent, down_proj.T, preferred_element_type=jnp.float32)
    grad_in = grad_out.astype(jnp.float32) + row_scale * grad_normed - values * row_scale ** 3 * lax.optimization_barrier(jnp.mean(values * grad_normed, axis=-1, keepdims=True))
    return (grad_in.astype(jnp.bfloat16), normed, latent_act, grad_latent)

def adamw(master, moment1, moment2, gradient):
    first_new = first_decay * moment1.astype(jnp.float32) + (1.0 - first_decay) * gradient
    second_new = second_decay * moment2.astype(jnp.float32) + (1.0 - second_decay) * gradient * gradient
    first_hat = first_new / (1.0 - first_decay ** step_count)
    second_hat = second_new / (1.0 - second_decay ** step_count)
    updated = master - learn_rate * (first_hat / (jnp.sqrt(second_hat) + adam_epsilon) + weight_decay * master)
    return (updated, first_new.astype(jnp.bfloat16), second_new.astype(jnp.bfloat16))

def direction_partials(saved, cotangent, weights, travel_sense):
    sections = saved.shape[0]
    micro_count = saved.shape[2]
    features = saved.shape[4]

    def visit(grad_out, section):
        holder = section if travel_sense == 0 else sections - 1 - section
        inputs = lax.dynamic_index_in_dim(saved, holder, 0, keepdims=False)[travel_sense]
        section_weights = lax.dynamic_index_in_dim(weights, holder, 0, keepdims=False)[travel_sense]
        grad_in, normed, latent_act, grad_latent = section_backward(inputs.reshape(-1, features), grad_out.reshape(-1, features), section_weights)
        latent_width = grad_latent.shape[-1]
        normed_split = normed.reshape(micro_count, N_DP, -1, features).astype(jnp.float32)
        latent_split = grad_latent.reshape(micro_count, N_DP, -1, latent_width).astype(jnp.float32)
        out_split = grad_out.reshape(micro_count, N_DP, -1, features).astype(jnp.float32)
        act_split = latent_act.reshape(micro_count, N_DP, -1, latent_width).astype(jnp.float32)
        down_part = jnp.einsum('mptd,mptk->pdk', normed_split, latent_split)
        up_part = jnp.einsum('mptd,mptk->pdk', out_split, act_split)
        rounded = jnp.concatenate([down_part, up_part], axis=-1).astype(jnp.bfloat16)
        rounded = lax.optimization_barrier(rounded)
        return (grad_in.reshape(grad_out.shape), lax.optimization_barrier(jnp.sum(rounded.astype(jnp.float32), axis=0)))
    section_order = jnp.arange(sections - 1, -1, -1, dtype=jnp.int32)
    _, partials = lax.scan(visit, cotangent[travel_sense], section_order)
    return partials[::-1]

def reference(weights, master, moment1, moment2, saved, cotangent):
    gradient = direction_partials(saved, cotangent, weights, 0) + direction_partials(saved, cotangent, weights, 1)
    new_master, new_first, new_second = adamw(master, moment1, moment2, gradient)
    return (new_master, new_first, new_second)
```

```python
import jax
import jax.numpy as jnp
from jax import lax
from jax.sharding import PartitionSpec as P

norm_epsilon = 1e-06
first_decay = 0.9
second_decay = 0.95
adam_epsilon = 1e-08
learn_rate = 0.00022
weight_decay = 0.1
step_count = 100.0


def adamw(master, moment1, moment2, gradient):
    first_new = first_decay * moment1.astype(jnp.float32) + (1.0 - first_decay) * gradient
    second_new = (
        second_decay * moment2.astype(jnp.float32) + (1.0 - second_decay) * gradient * gradient
    )
    first_hat = first_new / (1.0 - first_decay**step_count)
    second_hat = second_new / (1.0 - second_decay**step_count)
    updated = master - learn_rate * (
        first_hat / (jnp.sqrt(second_hat) + adam_epsilon) + weight_decay * master
    )
    return (updated, first_new.astype(jnp.bfloat16), second_new.astype(jnp.bfloat16))


def prepare(x, down_proj):
    values = x.astype(jnp.float32)
    row_scale = lax.rsqrt(jnp.mean(values * values, axis=-1, keepdims=True) + norm_epsilon)
    normed = (values * row_scale).astype(jnp.bfloat16)
    latent = jnp.einsum("mtd,dk->mtk", normed, down_proj, preferred_element_type=jnp.float32)
    return row_scale, normed, latent


def replica_pieces(array):
    count = lax.axis_size("dp")
    me = lax.axis_index("dp")
    width = array.shape[-1] // count

    def piece(owner):
        return lax.dynamic_slice_in_dim(array, owner * width, width, array.ndim - 1)

    pieces = [piece(me)]
    for apart in range(1, count):
        pairs = [(i, (i + apart) % count) for i in range(count)]
        pieces.append(lax.ppermute(piece(lax.rem(me + apart, count)), "dp", pairs))
    return pieces


def replica_rows(array):
    count = lax.axis_size("dp")
    rows = [array]
    for apart in range(1, count):
        pairs = [(i, (i + apart) % count) for i in range(count)]
        rows.append(lax.ppermute(array, "dp", pairs))
    return rows


def shards(weights, master, moment1, moment2, saved, cotangent):
    sections = lax.axis_size("pipe")
    position = lax.axis_index("pipe")
    micro, rows, features = saved.shape[2:]
    section_weights = weights[0, 0]
    rank = section_weights.shape[1] // 2
    down_proj = section_weights[:, :rank]
    up_proj = section_weights[:, rank:]

    swap = [(i, sections - 1 - i) for i in range(sections)]
    x_ahead = saved[0, 0]
    x_behind = lax.ppermute(saved[0, 1], "pipe", swap)
    scale_a, normed_a, latent_a = prepare(x_ahead, down_proj)
    scale_b, normed_b, latent_b = prepare(x_behind, down_proj)
    x = jnp.concatenate([x_ahead, x_behind], axis=1)
    row_scale = jnp.concatenate([scale_a, scale_b], axis=1)
    latent = jnp.concatenate([latent_a, latent_b], axis=1)
    latent_scale = lax.rsqrt(jnp.mean(latent * latent, axis=-1, keepdims=True) + norm_epsilon)
    latent_act = (latent * latent_scale).astype(jnp.bfloat16)
    entries = jnp.concatenate([cotangent[0], cotangent[1]], axis=1)

    down_pairs = [(i, i - 1) for i in range(1, sections)]
    first_tick = sections - 1 - position
    received, latents = [], []
    sent = None
    for tick in range(sections - 1 + micro):
        index = jnp.clip(tick - first_tick, 0, micro - 1)

        def at(array):
            return lax.dynamic_index_in_dim(array, index, 0, keepdims=False)

        if sent is None:
            grad_out = entries[0]
        else:
            grad_out = lax.ppermute(sent, "pipe", down_pairs)
            if tick < micro:
                grad_out = jnp.where(position == sections - 1, entries[tick], grad_out)
        x_now, scale_now, latent_now, lscale_now = at(x), at(row_scale), at(latent), at(latent_scale)
        grad_act = jnp.dot(grad_out, up_proj, preferred_element_type=jnp.float32)
        grad_latent = lscale_now * grad_act - latent_now * lscale_now**3 * jnp.mean(
            latent_now * grad_act, axis=-1, keepdims=True
        )
        grad_latent = grad_latent.astype(jnp.bfloat16)
        along = jnp.sum(latent_now * grad_latent.astype(jnp.float32), axis=-1, keepdims=True)
        along = along * (scale_now * scale_now / features)
        grad_normed = jnp.dot(grad_latent, down_proj.T, preferred_element_type=jnp.float32)
        sent = (
            grad_out.astype(jnp.float32)
            + scale_now * grad_normed
            - x_now.astype(jnp.float32) * along
        ).astype(jnp.bfloat16)
        received.append(grad_out)
        latents.append(grad_latent)

    grad_out = lax.dynamic_slice_in_dim(jnp.stack(received), first_tick, micro, 0)
    grad_latent = lax.dynamic_slice_in_dim(jnp.stack(latents), first_tick, micro, 0)

    def flat(array):
        return array.reshape(-1, array.shape[-1])

    normed = jnp.concatenate([normed_a, normed_b], axis=1)
    normed_all = jnp.concatenate(replica_pieces(flat(normed)))
    narrow = jnp.concatenate([flat(grad_latent), flat(latent_act)], axis=1)
    narrow_all = jnp.concatenate(replica_rows(narrow))
    wide_all = jnp.concatenate(replica_pieces(flat(grad_out)))
    down_part = jnp.einsum("td,tk->dk", normed_all, narrow_all[:, :rank], preferred_element_type=jnp.float32)
    up_part = jnp.einsum("td,tk->dk", wide_all, narrow_all[:, rank:], preferred_element_type=jnp.float32)
    gradient = jnp.concatenate([down_part, up_part], axis=1)
    new_master, new_first, new_second = adamw(master[0], moment1[0], moment2[0], gradient)
    return (new_master[None], new_first[None], new_second[None])


def solution(mesh):
    return jax.shard_map(
        shards,
        mesh=mesh,
        in_specs=(
            P("pipe", None, None, None),
            P("pipe", "dp", None),
            P("pipe", "dp", None),
            P("pipe", "dp", None),
            P("pipe", None, None, "dp", None),
            P(None, None, "dp", None),
        ),
        out_specs=(P("pipe", "dp", None), P("pipe", "dp", None), P("pipe", "dp", None)),
        check_vma=False,
    )
```

```python
import functools

import jax
import jax.numpy as jnp
from jax import lax
from jax.experimental import pallas as pl
from jax.experimental.pallas import tpu as pltpu
from jax.sharding import PartitionSpec as P

norm_epsilon = 1e-06
first_decay = 0.9
second_decay = 0.95
adam_epsilon = 1e-08
learn_rate = 0.00022
weight_decay = 0.1
step_count = 100.0


def adamw(master, moment1, moment2, gradient):
    first_new = first_decay * moment1.astype(jnp.float32) + (1.0 - first_decay) * gradient
    second_new = (
        second_decay * moment2.astype(jnp.float32) + (1.0 - second_decay) * gradient * gradient
    )
    first_hat = first_new / (1.0 - first_decay**step_count)
    second_hat = second_new / (1.0 - second_decay**step_count)
    updated = master - learn_rate * (
        first_hat / (jnp.sqrt(second_hat) + adam_epsilon) + weight_decay * master
    )
    return (updated, first_new.astype(jnp.bfloat16), second_new.astype(jnp.bfloat16))


def chain_kernel(
    n_dp, sections, weights_ref, saved_ref, cot_ref,
    normed_all, wide_all, narrow_all,
    w, arrived, outgoing, swapped, normed_cut, wide_cut, latents, scales,
    w_sem, ex_send, ex_recv, chain_send, chain_recv, swap_send, swap_recv,
):
    me = lax.axis_index("dp")
    position = lax.axis_index("pipe")
    pieces, rows, features = saved_ref.shape
    half = pieces // 2
    rank = w.shape[1] // 2
    cut = features // n_dp
    partner = sections - 1 - position
    below = lax.rem(position + sections - 1, sections)
    above = lax.rem(position + 1, sections)

    w_copy = pltpu.make_async_copy(weights_ref.at[0], w, w_sem)
    w_copy.start()

    barrier = pltpu.get_barrier_semaphore()

    def greet(device):
        pl.semaphore_signal(
            barrier, inc=1, device_id=device, device_id_type=pl.DeviceIdType.MESH
        )

    for apart in range(1, n_dp):
        greet({"dp": lax.rem(me + apart, n_dp)})
    for device in (partner, below, above):
        greet({"pipe": device})
    pl.semaphore_wait(barrier, n_dp + 2)

    def remote(source, target, send, receive, device):
        return pltpu.make_async_remote_copy(
            src_ref=source, dst_ref=target, send_sem=send, recv_sem=receive,
            device_id=device, device_id_type=pl.DeviceIdType.MESH,
        )

    def swap_copy(h):
        return remote(
            saved_ref.at[half + h], swapped.at[h], swap_send.at[h], swap_recv.at[h],
            {"pipe": partner},
        )

    def chain_copy(k):
        return remote(
            outgoing.at[k], arrived.at[k], chain_send.at[k], chain_recv.at[k], {"pipe": below}
        )

    def exchange(kind, apart, k):
        peer = lax.rem(me + apart, n_dp)
        target = (normed_all, wide_all, narrow_all)[kind]
        source = (
            normed_cut.at[peer, k], wide_cut.at[peer, k], narrow_all.at[0, k]
        )[kind]
        return remote(
            source, target.at[apart, k], ex_send.at[kind, apart, k],
            ex_recv.at[kind, apart, k], {"dp": peer},
        )

    for h in range(half):
        swap_copy(h).start()
    w_copy.wait()

    def prepare(k):
        if k < half:
            x = saved_ref[k]
        else:
            swap_copy(k - half).wait_recv()
            x = swapped[k - half]
        values = x.astype(jnp.float32)
        row_scale = lax.rsqrt(jnp.mean(values * values, axis=-1, keepdims=True) + norm_epsilon)
        normed = (values * row_scale).astype(jnp.bfloat16)
        latent = jnp.dot(normed, w[:, :rank], preferred_element_type=jnp.float32)
        latents[k] = latent
        scales[k] = jnp.broadcast_to(row_scale, scales.shape[1:])
        latent_scale = lax.rsqrt(jnp.mean(latent * latent, axis=-1, keepdims=True) + norm_epsilon)
        narrow_all[0, k, :, rank:] = (latent * latent_scale).astype(jnp.bfloat16)
        for owner in range(n_dp):
            normed_cut[owner, k] = normed[:, owner * cut : (owner + 1) * cut]
        for apart in range(1, n_dp):
            exchange(0, apart, k).start()
        normed_all[0, k] = normed_cut[me, k]

    def advance(k):
        @pl.when(position == sections - 1)
        def _():
            arrived[k] = cot_ref[k]

        @pl.when(position < sections - 1)
        def _():
            chain_copy(k).wait_recv()

        grad_out = arrived[k]
        latent = latents[k]
        row_scale = scales[k][:, :1]
        latent_scale = lax.rsqrt(jnp.mean(latent * latent, axis=-1, keepdims=True) + norm_epsilon)
        grad_act = jnp.dot(grad_out, w[:, rank:], preferred_element_type=jnp.float32)
        grad_latent = latent_scale * grad_act - latent * latent_scale**3 * jnp.mean(
            latent * grad_act, axis=-1, keepdims=True
        )
        grad_latent = grad_latent.astype(jnp.bfloat16)
        narrow_all[0, k, :, :rank] = grad_latent

        @pl.when(position > 0)
        def _():
            along = jnp.sum(latent * grad_latent.astype(jnp.float32), axis=-1, keepdims=True)
            along = along * (row_scale * row_scale / features)
            x = saved_ref[k] if k < half else swapped[k - half]
            grad_normed = lax.dot_general(
                grad_latent, w[:, :rank], (((1,), (1,)), ((), ())),
                preferred_element_type=jnp.float32,
            )
            outgoing[k] = (
                arrived[k].astype(jnp.float32)
                + row_scale * grad_normed
                - x.astype(jnp.float32) * along
            ).astype(jnp.bfloat16)
            chain_copy(k).start()

        for owner in range(n_dp):
            wide_cut[owner, k] = arrived[k, :, owner * cut : (owner + 1) * cut]
        for apart in range(1, n_dp):
            exchange(1, apart, k).start()
            exchange(2, apart, k).start()
        wide_all[0, k] = wide_cut[me, k]

    for k in range(half):
        prepare(k)
    for k in range(half):
        advance(k)
    for k in range(half, pieces):
        prepare(k)
        advance(k)

    for h in range(half):
        swap_copy(h).wait_send()

    @pl.when(position > 0)
    def _():
        for k in range(pieces):
            chain_copy(k).wait_send()

    for kind in range(3):
        for apart in range(1, n_dp):
            for k in range(pieces):
                exchange(kind, apart, k).wait()


def shards(weights, master, moment1, moment2, saved, cotangent):
    n_dp = lax.axis_size("dp")
    sections = lax.axis_size("pipe")
    micro, batch_rows, features = saved.shape[2:]
    width = weights.shape[3]
    rank = width // 2
    pieces = micro
    rows = 2 * micro * batch_rows // pieces
    cut = features // n_dp
    bf16, f32 = jnp.bfloat16, jnp.float32
    vmem = pl.BlockSpec(memory_space=pltpu.VMEM)
    flops = 2 * pieces * rows * features * rank * 3
    normed_all, wide_all, narrow_all = pl.pallas_call(
        functools.partial(chain_kernel, n_dp, sections),
        out_shape=[
            jax.ShapeDtypeStruct((n_dp, pieces, rows, cut), bf16),
            jax.ShapeDtypeStruct((n_dp, pieces, rows, cut), bf16),
            jax.ShapeDtypeStruct((n_dp, pieces, rows, width), bf16),
        ],
        in_specs=[pl.BlockSpec(memory_space=pl.ANY), vmem, vmem],
        out_specs=[vmem, vmem, vmem],
        scratch_shapes=[
            pltpu.VMEM((features, width), bf16),
            pltpu.VMEM((pieces, rows, features), bf16),
            pltpu.VMEM((pieces, rows, features), bf16),
            pltpu.VMEM((pieces // 2, rows, features), bf16),
            pltpu.VMEM((n_dp, pieces, rows, cut), bf16),
            pltpu.VMEM((n_dp, pieces, rows, cut), bf16),
            pltpu.VMEM((pieces, rows, rank), f32),
            pltpu.VMEM((pieces, rows, 128), f32),
            pltpu.SemaphoreType.DMA,
            pltpu.SemaphoreType.DMA((3, n_dp, pieces)),
            pltpu.SemaphoreType.DMA((3, n_dp, pieces)),
            pltpu.SemaphoreType.DMA((pieces,)),
            pltpu.SemaphoreType.DMA((pieces,)),
            pltpu.SemaphoreType.DMA((pieces // 2,)),
            pltpu.SemaphoreType.DMA((pieces // 2,)),
        ],
        compiler_params=pltpu.CompilerParams(
            collective_id=0, has_side_effects=True, vmem_limit_bytes=44 * 2**20
        ),
        cost_estimate=pl.CostEstimate(
            flops=flops, bytes_accessed=features * width * 2, transcendentals=0
        ),
    )(
        weights.reshape(2, features, width),
        saved.reshape(pieces, rows, features),
        cotangent.reshape(pieces, rows, features),
    )
    normed_all = normed_all.reshape(-1, cut)
    wide_all = wide_all.reshape(-1, cut)
    narrow_all = narrow_all.reshape(-1, width)
    down_part = jnp.einsum("td,tk->dk", normed_all, narrow_all[:, :rank], preferred_element_type=f32)
    up_part = jnp.einsum("td,tk->dk", wide_all, narrow_all[:, rank:], preferred_element_type=f32)
    gradient = jnp.concatenate([down_part, up_part], axis=1)
    new_master, new_first, new_second = adamw(master[0], moment1[0], moment2[0], gradient)
    return (new_master[None], new_first[None], new_second[None])


def solution(mesh):
    return jax.shard_map(
        shards,
        mesh=mesh,
        in_specs=(
            P("pipe", None, None, None),
            P("pipe", "dp", None),
            P("pipe", "dp", None),
            P("pipe", "dp", None),
            P("pipe", None, None, "dp", None),
            P(None, None, "dp", None),
        ),
        out_specs=(P("pipe", "dp", None), P("pipe", "dp", None), P("pipe", "dp", None)),
        check_vma=False,
    )
```

```python
import functools

import jax
import jax.numpy as jnp
from jax import lax
from jax.experimental import pallas as pl
from jax.experimental.pallas import tpu as pltpu
from jax.sharding import PartitionSpec as P

norm_epsilon = 1e-06
first_decay = 0.9
second_decay = 0.95
adam_epsilon = 1e-08
learn_rate = 0.00022
weight_decay = 0.1
step_count = 100.0


def adamw(master, moment1, moment2, gradient):
    first_new = first_decay * moment1.astype(jnp.float32) + (1.0 - first_decay) * gradient
    second_new = (
        second_decay * moment2.astype(jnp.float32) + (1.0 - second_decay) * gradient * gradient
    )
    first_hat = first_new / (1.0 - first_decay**step_count)
    second_hat = second_new / (1.0 - second_decay**step_count)
    updated = master - learn_rate * (
        first_hat / (jnp.sqrt(second_hat) + adam_epsilon) + weight_decay * master
    )
    return (updated, first_new.astype(jnp.bfloat16), second_new.astype(jnp.bfloat16))


def chain_kernel(
    n_dp, sections, weights_ref, saved_ref, cot_ref,
    normed_all, wide_all, narrow_all,
    w, here, arrived, outgoing, swapped, normed_cut, wide_cut, latents, scales,
    w_sem, here_sem, cot_sem, ex_send, ex_recv, chain_send, chain_recv, swap_send, swap_recv,
    turn,
):
    me = lax.axis_index("dp")
    position = lax.axis_index("pipe")
    pieces, rows, features = saved_ref.shape
    half = pieces // 2
    rank = w.shape[1] // 2
    cut = features // n_dp
    chunks = chain_send.shape[1]
    chunk = features // chunks
    columns = [pl.ds(c * chunk, chunk) for c in range(chunks)]
    lower = sections // 2
    late = lower + sections // 4
    partner = sections - 1 - position
    below = lax.rem(position + sections - 1, sections)
    above = lax.rem(position + 1, sections)

    w_copy = pltpu.make_async_copy(weights_ref.at[0], w, w_sem)
    w_copy.start()
    here_copy = pltpu.make_async_copy(saved_ref.at[pl.ds(0, half)], here, here_sem)
    here_copy.start()
    cot_copy = pltpu.make_async_copy(cot_ref, arrived, cot_sem)

    @pl.when(position == sections - 1)
    def _():
        cot_copy.start()

    barrier = pltpu.get_barrier_semaphore()

    def greet(device):
        pl.semaphore_signal(
            barrier, inc=1, device_id=device, device_id_type=pl.DeviceIdType.MESH
        )

    for apart in range(1, n_dp):
        greet({"dp": lax.rem(me + apart, n_dp)})
    for device in (partner, below, above):
        greet({"pipe": device})
    pl.semaphore_wait(barrier, n_dp + 2)

    def remote(source, target, send, receive, device):
        return pltpu.make_async_remote_copy(
            src_ref=source, dst_ref=target, send_sem=send, recv_sem=receive,
            device_id=device, device_id_type=pl.DeviceIdType.MESH,
        )

    def swap_copy(h, c):
        return remote(
            saved_ref.at[half + h, :, columns[c]], swapped.at[h, :, columns[c]],
            swap_send.at[h, c], swap_recv.at[h, c], {"pipe": partner},
        )

    def swap_each(act):
        for h in range(half):
            for c in range(chunks):
                act(swap_copy(h, c))

    def chain_copy(k, c):
        return remote(
            outgoing.at[k, :, columns[c]], arrived.at[k, :, columns[c]],
            chain_send.at[k, c], chain_recv.at[k, c], {"pipe": below},
        )

    def exchange(kind, apart, k):
        peer = lax.rem(me + apart, n_dp)
        target = (normed_all, wide_all, narrow_all)[kind]
        source = (
            normed_cut.at[peer, k], wide_cut.at[peer, k], narrow_all.at[0, k]
        )[kind]
        return remote(
            source, target.at[apart, k], ex_send.at[kind, apart, k],
            ex_recv.at[kind, apart, k], {"dp": peer},
        )

    @pl.when((position == 0) | ((position >= lower) & (position < late)))
    def _():
        swap_each(lambda copy: copy.start())

    here_copy.wait()
    w_copy.wait()

    def prepare(k):
        if k < half:
            x = here[k]
        else:
            for c in range(chunks):
                swap_copy(k - half, c).wait_recv()
            x = swapped[k - half]
        values = x.astype(jnp.float32)
        row_scale = lax.rsqrt(jnp.mean(values * values, axis=-1, keepdims=True) + norm_epsilon)
        normed = (values * row_scale).astype(jnp.bfloat16)
        latent = jnp.dot(normed, w[:, :rank], preferred_element_type=jnp.float32)
        latents[k] = latent
        scales[k] = jnp.broadcast_to(row_scale, scales.shape[1:])
        latent_scale = lax.rsqrt(jnp.mean(latent * latent, axis=-1, keepdims=True) + norm_epsilon)
        narrow_all[0, k, :, rank:] = (latent * latent_scale).astype(jnp.bfloat16)
        for owner in range(n_dp):
            normed_cut[owner, k] = normed[:, owner * cut : (owner + 1) * cut]
        for apart in range(1, n_dp):
            exchange(0, apart, k).start()
        normed_all[0, k] = normed_cut[me, k]

    def advance(k):
        @pl.when(position == sections - 1)
        def _():
            if k == 0:
                cot_copy.wait()

        latent = latents[k]
        row_scale = scales[k][:, :1]
        latent_scale = lax.rsqrt(jnp.mean(latent * latent, axis=-1, keepdims=True) + norm_epsilon)
        grad_act = jnp.zeros((rows, rank), jnp.float32)
        for c in range(chunks):

            @pl.when(position < sections - 1)
            def _():
                chain_copy(k, c).wait_recv()

            grad_act += jnp.dot(
                arrived[k, :, columns[c]], w[columns[c], rank:],
                preferred_element_type=jnp.float32,
            )
        grad_latent = latent_scale * grad_act - latent * latent_scale**3 * jnp.mean(
            latent * grad_act, axis=-1, keepdims=True
        )
        grad_latent = grad_latent.astype(jnp.bfloat16)
        narrow_all[0, k, :, :rank] = grad_latent

        @pl.when(position > 0)
        def _():
            along = jnp.sum(latent * grad_latent.astype(jnp.float32), axis=-1, keepdims=True)
            along = along * (row_scale * row_scale / features)
            x_ref = here.at[k] if k < half else swapped.at[k - half]
            for c in range(chunks):
                grad_normed = lax.dot_general(
                    grad_latent, w[columns[c], :rank], (((1,), (1,)), ((), ())),
                    preferred_element_type=jnp.float32,
                )
                outgoing[k, :, columns[c]] = (
                    arrived[k, :, columns[c]].astype(jnp.float32)
                    + row_scale * grad_normed
                    - x_ref[:, columns[c]].astype(jnp.float32) * along
                ).astype(jnp.bfloat16)
                chain_copy(k, c).start()

        for owner in range(n_dp):
            wide_cut[owner, k] = arrived[k, :, owner * cut : (owner + 1) * cut]
        for apart in range(1, n_dp):
            exchange(1, apart, k).start()
            exchange(2, apart, k).start()
        wide_all[0, k] = wide_cut[me, k]

    for k in range(half):
        prepare(k)

    @pl.when((position > 0) & (position < lower))
    def _():
        pl.semaphore_wait(turn, 1)
        swap_each(lambda copy: copy.start())

    @pl.when(position < lower - 1)
    def _():
        swap_each(lambda copy: copy.wait_send())
        pl.semaphore_signal(
            turn, inc=1, device_id={"pipe": above}, device_id_type=pl.DeviceIdType.MESH
        )

    for k in range(half):
        advance(k)
    for k in range(half, pieces):
        prepare(k)
        advance(k)

    @pl.when(position >= late)
    def _():
        swap_each(lambda copy: copy.start())

    @pl.when(position >= lower - 1)
    def _():
        swap_each(lambda copy: copy.wait_send())

    @pl.when(position > 0)
    def _():
        for k in range(pieces):
            for c in range(chunks):
                chain_copy(k, c).wait_send()

    for kind in range(3):
        for apart in range(1, n_dp):
            for k in range(pieces):
                exchange(kind, apart, k).wait()


def shards(weights, master, moment1, moment2, saved, cotangent):
    n_dp = lax.axis_size("dp")
    sections = lax.axis_size("pipe")
    micro, batch_rows, features = saved.shape[2:]
    width = weights.shape[3]
    rank = width // 2
    pieces = micro
    rows = 2 * micro * batch_rows // pieces
    cut = features // n_dp
    chunks = 5 if features % (5 * 128) == 0 else 1
    bf16, f32 = jnp.bfloat16, jnp.float32
    vmem = pl.BlockSpec(memory_space=pltpu.VMEM)
    flops = 2 * pieces * rows * features * rank * 3
    normed_all, wide_all, narrow_all = pl.pallas_call(
        functools.partial(chain_kernel, n_dp, sections),
        out_shape=[
            jax.ShapeDtypeStruct((n_dp, pieces, rows, cut), bf16),
            jax.ShapeDtypeStruct((n_dp, pieces, rows, cut), bf16),
            jax.ShapeDtypeStruct((n_dp, pieces, rows, width), bf16),
        ],
        in_specs=[pl.BlockSpec(memory_space=pl.ANY)] * 3,
        out_specs=[vmem, vmem, vmem],
        scratch_shapes=[
            pltpu.VMEM((features, width), bf16),
            pltpu.VMEM((pieces // 2, rows, features), bf16),
            pltpu.VMEM((pieces, rows, features), bf16),
            pltpu.VMEM((pieces, rows, features), bf16),
            pltpu.VMEM((pieces // 2, rows, features), bf16),
            pltpu.VMEM((n_dp, pieces, rows, cut), bf16),
            pltpu.VMEM((n_dp, pieces, rows, cut), bf16),
            pltpu.VMEM((pieces, rows, rank), f32),
            pltpu.VMEM((pieces, rows, 128), f32),
            pltpu.SemaphoreType.DMA,
            pltpu.SemaphoreType.DMA,
            pltpu.SemaphoreType.DMA,
            pltpu.SemaphoreType.DMA((3, n_dp, pieces)),
            pltpu.SemaphoreType.DMA((3, n_dp, pieces)),
            pltpu.SemaphoreType.DMA((pieces, chunks)),
            pltpu.SemaphoreType.DMA((pieces, chunks)),
            pltpu.SemaphoreType.DMA((pieces // 2, chunks)),
            pltpu.SemaphoreType.DMA((pieces // 2, chunks)),
            pltpu.SemaphoreType.REGULAR,
        ],
        compiler_params=pltpu.CompilerParams(
            collective_id=0, has_side_effects=True, vmem_limit_bytes=44 * 2**20
        ),
        cost_estimate=pl.CostEstimate(
            flops=flops, bytes_accessed=features * width * 2, transcendentals=0
        ),
    )(
        weights.reshape(2, features, width),
        saved.reshape(pieces, rows, features),
        cotangent.reshape(pieces, rows, features),
    )
    normed_all = normed_all.reshape(-1, cut)
    wide_all = wide_all.reshape(-1, cut)
    narrow_all = narrow_all.reshape(-1, width)
    down_part = jnp.einsum("td,tk->dk", normed_all, narrow_all[:, :rank], preferred_element_type=f32)
    up_part = jnp.einsum("td,tk->dk", wide_all, narrow_all[:, rank:], preferred_element_type=f32)
    gradient = jnp.concatenate([down_part, up_part], axis=1)
    new_master, new_first, new_second = adamw(master[0], moment1[0], moment2[0], gradient)
    return (new_master[None], new_first[None], new_second[None])


def solution(mesh):
    return jax.shard_map(
        shards,
        mesh=mesh,
        in_specs=(
            P("pipe", None, None, None),
            P("pipe", "dp", None),
            P("pipe", "dp", None),
            P("pipe", "dp", None),
            P("pipe", None, None, "dp", None),
            P(None, None, "dp", None),
        ),
        out_specs=(P("pipe", "dp", None), P("pipe", "dp", None), P("pipe", "dp", None)),
        check_vma=False,
    )
```

```python
import functools

import jax
import jax.numpy as jnp
from jax import lax
from jax.experimental import pallas as pl
from jax.experimental.pallas import tpu as pltpu
from jax.sharding import PartitionSpec as P

norm_epsilon = 1e-06
first_decay = 0.9
second_decay = 0.95
adam_epsilon = 1e-08
learn_rate = 0.00022
weight_decay = 0.1
step_count = 100.0


def adamw(master, moment1, moment2, gradient):
    first_new = first_decay * moment1.astype(jnp.float32) + (1.0 - first_decay) * gradient
    second_new = (
        second_decay * moment2.astype(jnp.float32) + (1.0 - second_decay) * gradient * gradient
    )
    first_hat = first_new / (1.0 - first_decay**step_count)
    second_hat = second_new / (1.0 - second_decay**step_count)
    updated = master - learn_rate * (
        first_hat / (jnp.sqrt(second_hat) + adam_epsilon) + weight_decay * master
    )
    return (updated, first_new.astype(jnp.bfloat16), second_new.astype(jnp.bfloat16))


def chain_kernel(
    n_dp, sections, weights_ref, saved_ref, cot_ref,
    normed_all, wide_all, narrow_all,
    w, here, arrived, outgoing, swapped, normed_cut, wide_cut, latents, scales,
    w_sem, here_sem, cot_sem, ex_send, ex_recv, chain_send, chain_recv, swap_send, swap_recv,
    turn,
):
    me = lax.axis_index("dp")
    position = lax.axis_index("pipe")
    pieces, rows, features = saved_ref.shape
    half = pieces // 2
    rank = w.shape[1] // 2
    cut = features // n_dp
    chunks = chain_send.shape[1]
    chunk = features // chunks
    columns = [pl.ds(c * chunk, chunk) for c in range(chunks)]
    lower = sections // 2
    late = lower + sections // 4
    partner = sections - 1 - position
    below = lax.rem(position + sections - 1, sections)
    above = lax.rem(position + 1, sections)

    w_copy = pltpu.make_async_copy(weights_ref.at[0], w, w_sem)
    w_copy.start()
    here_copy = pltpu.make_async_copy(saved_ref.at[pl.ds(0, half)], here, here_sem)
    here_copy.start()
    cot_copy = pltpu.make_async_copy(cot_ref, arrived, cot_sem)

    @pl.when(position == sections - 1)
    def _():
        cot_copy.start()

    barrier = pltpu.get_barrier_semaphore()

    def greet(device):
        pl.semaphore_signal(
            barrier, inc=1, device_id=device, device_id_type=pl.DeviceIdType.MESH
        )

    for apart in range(1, n_dp):
        greet({"dp": lax.rem(me + apart, n_dp)})
    for device in (partner, below, above):
        greet({"pipe": device})
    pl.semaphore_wait(barrier, n_dp + 2)

    def remote(source, target, send, receive, device):
        return pltpu.make_async_remote_copy(
            src_ref=source, dst_ref=target, send_sem=send, recv_sem=receive,
            device_id=device, device_id_type=pl.DeviceIdType.MESH,
        )

    def swap_copy(h, c):
        return remote(
            saved_ref.at[half + h, :, columns[c]], swapped.at[h, :, columns[c]],
            swap_send.at[h, c], swap_recv.at[h, c], {"pipe": partner},
        )

    def swap_each(act):
        for h in range(half):
            for c in range(chunks):
                act(swap_copy(h, c))

    def chain_copy(k, c):
        return remote(
            outgoing.at[k, :, columns[c]], arrived.at[k, :, columns[c]],
            chain_send.at[k, c], chain_recv.at[k, c], {"pipe": below},
        )

    def exchange(kind, apart, k):
        peer = lax.rem(me + apart, n_dp)
        target = (normed_all, wide_all, narrow_all)[kind]
        source = (
            normed_cut.at[peer, k], wide_cut.at[peer, k], narrow_all.at[0, k]
        )[kind]
        return remote(
            source, target.at[apart, k], ex_send.at[kind, apart, k],
            ex_recv.at[kind, apart, k], {"dp": peer},
        )

    @pl.when((position == 0) | ((position >= lower) & (position < late)))
    def _():
        swap_each(lambda copy: copy.start())

    here_copy.wait()
    w_copy.wait()

    def prepare(k):
        if k < half:
            x = here[k]
        else:
            for c in range(chunks):
                swap_copy(k - half, c).wait_recv()
            x = swapped[k - half]
        values = x.astype(jnp.float32)
        row_scale = lax.rsqrt(jnp.mean(values * values, axis=-1, keepdims=True) + norm_epsilon)
        normed = (values * row_scale).astype(jnp.bfloat16)
        latent = jnp.dot(normed, w[:, :rank], preferred_element_type=jnp.float32)
        latents[k] = latent
        scales[k] = jnp.broadcast_to(row_scale, scales.shape[1:])
        latent_scale = lax.rsqrt(jnp.mean(latent * latent, axis=-1, keepdims=True) + norm_epsilon)
        narrow_all[0, k, :, rank:] = (latent * latent_scale).astype(jnp.bfloat16)
        for owner in range(n_dp):
            normed_cut[owner, k] = normed[:, owner * cut : (owner + 1) * cut]
        for apart in range(1, n_dp):
            exchange(0, apart, k).start()
        normed_all[0, k] = normed_cut[me, k]

    def advance(k):
        @pl.when(position == sections - 1)
        def _():
            if k == 0:
                cot_copy.wait()

        latent = latents[k]
        row_scale = scales[k][:, :1]
        latent_scale = lax.rsqrt(jnp.mean(latent * latent, axis=-1, keepdims=True) + norm_epsilon)
        grad_act = jnp.zeros((rows, rank), jnp.float32)
        for c in range(chunks):

            @pl.when(position < sections - 1)
            def _():
                chain_copy(k, c).wait_recv()

            grad_act += jnp.dot(
                arrived[k, :, columns[c]], w[columns[c], rank:],
                preferred_element_type=jnp.float32,
            )
        grad_latent = latent_scale * grad_act - latent * latent_scale**3 * jnp.mean(
            latent * grad_act, axis=-1, keepdims=True
        )
        grad_latent = grad_latent.astype(jnp.bfloat16)
        narrow_all[0, k, :, :rank] = grad_latent

        @pl.when(position > 0)
        def _():
            along = jnp.sum(latent * grad_latent.astype(jnp.float32), axis=-1, keepdims=True)
            along = along * (row_scale * row_scale / features)
            x_ref = here.at[k] if k < half else swapped.at[k - half]
            for c in range(chunks):
                grad_normed = lax.dot_general(
                    grad_latent, w[columns[c], :rank], (((1,), (1,)), ((), ())),
                    preferred_element_type=jnp.float32,
                )
                outgoing[k, :, columns[c]] = (
                    arrived[k, :, columns[c]].astype(jnp.float32)
                    + row_scale * grad_normed
                    - x_ref[:, columns[c]].astype(jnp.float32) * along
                ).astype(jnp.bfloat16)
                chain_copy(k, c).start()

        for owner in range(n_dp):
            wide_cut[owner, k] = arrived[k, :, owner * cut : (owner + 1) * cut]
        for apart in range(1, n_dp):
            exchange(1, apart, k).start()
            exchange(2, apart, k).start()
        wide_all[0, k] = wide_cut[me, k]

    prepare(0)

    @pl.when((position > 0) & (position < lower))
    def _():
        pl.semaphore_wait(turn, 1)
        swap_each(lambda copy: copy.start())

    @pl.when(position < lower - 1)
    def _():
        swap_each(lambda copy: copy.wait_send())
        pl.semaphore_signal(
            turn, inc=1, device_id={"pipe": above}, device_id_type=pl.DeviceIdType.MESH
        )

    for k in range(pieces):
        advance(k)
        if k + 1 < pieces:
            prepare(k + 1)

    @pl.when(position >= late)
    def _():
        swap_each(lambda copy: copy.start())

    @pl.when(position >= lower - 1)
    def _():
        swap_each(lambda copy: copy.wait_send())

    @pl.when(position > 0)
    def _():
        for k in range(pieces):
            for c in range(chunks):
                chain_copy(k, c).wait_send()

    for kind in range(3):
        for apart in range(1, n_dp):
            for k in range(pieces):
                exchange(kind, apart, k).wait()


def shards(weights, master, moment1, moment2, saved, cotangent):
    n_dp = lax.axis_size("dp")
    sections = lax.axis_size("pipe")
    micro, batch_rows, features = saved.shape[2:]
    width = weights.shape[3]
    rank = width // 2
    pieces = 2 * micro
    rows = 2 * micro * batch_rows // pieces
    cut = features // n_dp
    chunks = 3 if features % (3 * 128) == 0 else 1
    bf16, f32 = jnp.bfloat16, jnp.float32
    vmem = pl.BlockSpec(memory_space=pltpu.VMEM)
    flops = 2 * pieces * rows * features * rank * 3
    normed_all, wide_all, narrow_all = pl.pallas_call(
        functools.partial(chain_kernel, n_dp, sections),
        out_shape=[
            jax.ShapeDtypeStruct((n_dp, pieces, rows, cut), bf16),
            jax.ShapeDtypeStruct((n_dp, pieces, rows, cut), bf16),
            jax.ShapeDtypeStruct((n_dp, pieces, rows, width), bf16),
        ],
        in_specs=[pl.BlockSpec(memory_space=pl.ANY)] * 3,
        out_specs=[vmem, vmem, vmem],
        scratch_shapes=[
            pltpu.VMEM((features, width), bf16),
            pltpu.VMEM((pieces // 2, rows, features), bf16),
            pltpu.VMEM((pieces, rows, features), bf16),
            pltpu.VMEM((pieces, rows, features), bf16),
            pltpu.VMEM((pieces // 2, rows, features), bf16),
            pltpu.VMEM((n_dp, pieces, rows, cut), bf16),
            pltpu.VMEM((n_dp, pieces, rows, cut), bf16),
            pltpu.VMEM((pieces, rows, rank), f32),
            pltpu.VMEM((pieces, rows, 128), f32),
            pltpu.SemaphoreType.DMA,
            pltpu.SemaphoreType.DMA,
            pltpu.SemaphoreType.DMA,
            pltpu.SemaphoreType.DMA((3, n_dp, pieces)),
            pltpu.SemaphoreType.DMA((3, n_dp, pieces)),
            pltpu.SemaphoreType.DMA((pieces, chunks)),
            pltpu.SemaphoreType.DMA((pieces, chunks)),
            pltpu.SemaphoreType.DMA((pieces // 2, chunks)),
            pltpu.SemaphoreType.DMA((pieces // 2, chunks)),
            pltpu.SemaphoreType.REGULAR,
        ],
        compiler_params=pltpu.CompilerParams(
            collective_id=0, has_side_effects=True, vmem_limit_bytes=44 * 2**20
        ),
        cost_estimate=pl.CostEstimate(
            flops=flops, bytes_accessed=features * width * 2, transcendentals=0
        ),
    )(
        weights.reshape(2, features, width),
        saved.reshape(pieces, rows, features),
        cotangent.reshape(pieces, rows, features),
    )
    normed_all = normed_all.reshape(-1, cut)
    wide_all = wide_all.reshape(-1, cut)
    narrow_all = narrow_all.reshape(-1, width)
    down_part = jnp.einsum("td,tk->dk", normed_all, narrow_all[:, :rank], preferred_element_type=f32)
    up_part = jnp.einsum("td,tk->dk", wide_all, narrow_all[:, rank:], preferred_element_type=f32)
    gradient = jnp.concatenate([down_part, up_part], axis=1)
    new_master, new_first, new_second = adamw(master[0], moment1[0], moment2[0], gradient)
    return (new_master[None], new_first[None], new_second[None])


def solution(mesh):
    return jax.shard_map(
        shards,
        mesh=mesh,
        in_specs=(
            P("pipe", None, None, None),
            P("pipe", "dp", None),
            P("pipe", "dp", None),
            P("pipe", "dp", None),
            P("pipe", None, None, "dp", None),
            P(None, None, "dp", None),
        ),
        out_specs=(P("pipe", "dp", None), P("pipe", "dp", None), P("pipe", "dp", None)),
        check_vma=False,
    )
```

```python
import functools

import jax
import jax.numpy as jnp
from jax import lax
from jax.experimental import pallas as pl
from jax.experimental.pallas import tpu as pltpu
from jax.sharding import PartitionSpec as P

norm_epsilon = 1e-06
first_decay = 0.9
second_decay = 0.95
adam_epsilon = 1e-08
learn_rate = 0.00022
weight_decay = 0.1
step_count = 100.0


def adamw(master, moment1, moment2, gradient):
    first_new = first_decay * moment1.astype(jnp.float32) + (1.0 - first_decay) * gradient
    second_new = (
        second_decay * moment2.astype(jnp.float32) + (1.0 - second_decay) * gradient * gradient
    )
    first_hat = first_new / (1.0 - first_decay**step_count)
    second_hat = second_new / (1.0 - second_decay**step_count)
    updated = master - learn_rate * (
        first_hat / (jnp.sqrt(second_hat) + adam_epsilon) + weight_decay * master
    )
    return (updated, first_new.astype(jnp.bfloat16), second_new.astype(jnp.bfloat16))


def chain_kernel(
    n_dp, sections, weights_ref, saved_ref, cot_ref,
    normed_all, wide_all, narrow_all,
    w, here, arrived, outgoing, swapped, normed_cut, wide_cut, latents, scales,
    w_sem, here_sem, cot_sem, ex_send, ex_recv, chain_send, chain_recv, swap_send, swap_recv,
    turn,
):
    me = lax.axis_index("dp")
    position = lax.axis_index("pipe")
    pieces, rows, features = saved_ref.shape
    half = pieces // 2
    rank = w.shape[1] // 2
    cut = features // n_dp
    chunks = chain_send.shape[1]
    chunk = features // chunks
    columns = [pl.ds(c * chunk, chunk) for c in range(chunks)]
    lower = sections // 2
    partner = sections - 1 - position
    below = lax.rem(position + sections - 1, sections)
    above = lax.rem(position + 1, sections)

    w_copy = pltpu.make_async_copy(weights_ref.at[0], w, w_sem)
    w_copy.start()
    here_copy = pltpu.make_async_copy(saved_ref.at[pl.ds(0, half)], here, here_sem)
    here_copy.start()
    cot_copy = pltpu.make_async_copy(cot_ref, arrived, cot_sem)

    @pl.when(position == sections - 1)
    def _():
        cot_copy.start()

    barrier = pltpu.get_barrier_semaphore()

    def greet(device):
        pl.semaphore_signal(
            barrier, inc=1, device_id=device, device_id_type=pl.DeviceIdType.MESH
        )

    for apart in range(1, n_dp):
        greet({"dp": lax.rem(me + apart, n_dp)})
    for device in (partner, below, above):
        greet({"pipe": device})
    pl.semaphore_wait(barrier, n_dp + 2)

    def remote(source, target, send, receive, device):
        return pltpu.make_async_remote_copy(
            src_ref=source, dst_ref=target, send_sem=send, recv_sem=receive,
            device_id=device, device_id_type=pl.DeviceIdType.MESH,
        )

    def swap_copy(h, c):
        return remote(
            saved_ref.at[half + h, :, columns[c]], swapped.at[h, :, columns[c]],
            swap_send.at[h, c], swap_recv.at[h, c], {"pipe": partner},
        )

    def swap_each(act):
        for h in range(half):
            for c in range(chunks):
                act(swap_copy(h, c))

    def chain_copy(k, c):
        return remote(
            outgoing.at[k, :, columns[c]], arrived.at[k, :, columns[c]],
            chain_send.at[k, c], chain_recv.at[k, c], {"pipe": below},
        )

    def exchange(kind, apart, k):
        peer = lax.rem(me + apart, n_dp)
        target = (normed_all, wide_all, narrow_all)[kind]
        source = (
            normed_cut.at[peer, k], wide_cut.at[peer, k], narrow_all.at[0, k]
        )[kind]
        return remote(
            source, target.at[apart, k], ex_send.at[kind, apart, k],
            ex_recv.at[kind, apart, k], {"dp": peer},
        )

    @pl.when((position == 0) | (position >= lower))
    def _():
        swap_each(lambda copy: copy.start())

    here_copy.wait()
    w_copy.wait()

    def prepare(k):
        if k < half:
            x = here[k]
        else:
            for c in range(chunks):
                swap_copy(k - half, c).wait_recv()
            x = swapped[k - half]
        values = x.astype(jnp.float32)
        row_scale = lax.rsqrt(jnp.mean(values * values, axis=-1, keepdims=True) + norm_epsilon)
        normed = (values * row_scale).astype(jnp.bfloat16)
        latent = jnp.dot(normed, w[:, :rank], preferred_element_type=jnp.float32)
        latents[k] = latent
        scales[k] = jnp.broadcast_to(row_scale, scales.shape[1:])
        latent_scale = lax.rsqrt(jnp.mean(latent * latent, axis=-1, keepdims=True) + norm_epsilon)
        narrow_all[0, k, :, rank:] = (latent * latent_scale).astype(jnp.bfloat16)
        for owner in range(n_dp):
            normed_cut[owner, k] = normed[:, owner * cut : (owner + 1) * cut]
        for apart in range(1, n_dp):
            exchange(0, apart, k).start()
        normed_all[0, k] = normed_cut[me, k]

    def advance(k):
        @pl.when(position == sections - 1)
        def _():
            if k == 0:
                cot_copy.wait()

        latent = latents[k]
        row_scale = scales[k][:, :1]
        latent_scale = lax.rsqrt(jnp.mean(latent * latent, axis=-1, keepdims=True) + norm_epsilon)
        grad_act = jnp.zeros((rows, rank), jnp.float32)
        for c in range(chunks):

            @pl.when(position < sections - 1)
            def _():
                chain_copy(k, c).wait_recv()

            grad_act += jnp.dot(
                arrived[k, :, columns[c]], w[columns[c], rank:],
                preferred_element_type=jnp.float32,
            )
        grad_latent = latent_scale * grad_act - latent * latent_scale**3 * jnp.mean(
            latent * grad_act, axis=-1, keepdims=True
        )
        grad_latent = grad_latent.astype(jnp.bfloat16)
        narrow_all[0, k, :, :rank] = grad_latent

        @pl.when(position > 0)
        def _():
            along = jnp.sum(latent * grad_latent.astype(jnp.float32), axis=-1, keepdims=True)
            along = along * (row_scale * row_scale / features)
            x_ref = here.at[k] if k < half else swapped.at[k - half]
            for c in range(chunks):
                grad_normed = lax.dot_general(
                    grad_latent, w[columns[c], :rank], (((1,), (1,)), ((), ())),
                    preferred_element_type=jnp.float32,
                )
                outgoing[k, :, columns[c]] = (
                    arrived[k, :, columns[c]].astype(jnp.float32)
                    + row_scale * grad_normed
                    - x_ref[:, columns[c]].astype(jnp.float32) * along
                ).astype(jnp.bfloat16)
                chain_copy(k, c).start()

        for owner in range(n_dp):
            wide_cut[owner, k] = arrived[k, :, owner * cut : (owner + 1) * cut]
        for apart in range(1, n_dp):
            exchange(1, apart, k).start()
            exchange(2, apart, k).start()
        wide_all[0, k] = wide_cut[me, k]

    prepare(0)

    @pl.when((position > 0) & (position < lower))
    def _():
        pl.semaphore_wait(turn, 1)
        swap_each(lambda copy: copy.start())

    @pl.when(position < lower - 1)
    def _():
        swap_each(lambda copy: copy.wait_send())
        pl.semaphore_signal(
            turn, inc=1, device_id={"pipe": above}, device_id_type=pl.DeviceIdType.MESH
        )

    for k in range(pieces):
        advance(k)
        if k + 1 < pieces:
            prepare(k + 1)

    @pl.when(position >= lower - 1)
    def _():
        swap_each(lambda copy: copy.wait_send())

    @pl.when(position > 0)
    def _():
        for k in range(pieces):
            for c in range(chunks):
                chain_copy(k, c).wait_send()

    for kind in range(3):
        for apart in range(1, n_dp):
            for k in range(pieces):
                exchange(kind, apart, k).wait()


def shards(weights, master, moment1, moment2, saved, cotangent):
    n_dp = lax.axis_size("dp")
    sections = lax.axis_size("pipe")
    micro, batch_rows, features = saved.shape[2:]
    width = weights.shape[3]
    rank = width // 2
    pieces = 2 * micro
    rows = 2 * micro * batch_rows // pieces
    cut = features // n_dp
    chunks = 3 if features % (3 * 128) == 0 else 1
    bf16, f32 = jnp.bfloat16, jnp.float32
    vmem = pl.BlockSpec(memory_space=pltpu.VMEM)
    flops = 2 * pieces * rows * features * rank * 3
    normed_all, wide_all, narrow_all = pl.pallas_call(
        functools.partial(chain_kernel, n_dp, sections),
        out_shape=[
            jax.ShapeDtypeStruct((n_dp, pieces, rows, cut), bf16),
            jax.ShapeDtypeStruct((n_dp, pieces, rows, cut), bf16),
            jax.ShapeDtypeStruct((n_dp, pieces, rows, width), bf16),
        ],
        in_specs=[pl.BlockSpec(memory_space=pl.ANY)] * 3,
        out_specs=[vmem, vmem, vmem],
        scratch_shapes=[
            pltpu.VMEM((features, width), bf16),
            pltpu.VMEM((pieces // 2, rows, features), bf16),
            pltpu.VMEM((pieces, rows, features), bf16),
            pltpu.VMEM((pieces, rows, features), bf16),
            pltpu.VMEM((pieces // 2, rows, features), bf16),
            pltpu.VMEM((n_dp, pieces, rows, cut), bf16),
            pltpu.VMEM((n_dp, pieces, rows, cut), bf16),
            pltpu.VMEM((pieces, rows, rank), f32),
            pltpu.VMEM((pieces, rows, 128), f32),
            pltpu.SemaphoreType.DMA,
            pltpu.SemaphoreType.DMA,
            pltpu.SemaphoreType.DMA,
            pltpu.SemaphoreType.DMA((3, n_dp, pieces)),
            pltpu.SemaphoreType.DMA((3, n_dp, pieces)),
            pltpu.SemaphoreType.DMA((pieces, chunks)),
            pltpu.SemaphoreType.DMA((pieces, chunks)),
            pltpu.SemaphoreType.DMA((pieces // 2, chunks)),
            pltpu.SemaphoreType.DMA((pieces // 2, chunks)),
            pltpu.SemaphoreType.REGULAR,
        ],
        compiler_params=pltpu.CompilerParams(
            collective_id=0, has_side_effects=True, vmem_limit_bytes=44 * 2**20
        ),
        cost_estimate=pl.CostEstimate(
            flops=flops, bytes_accessed=features * width * 2, transcendentals=0
        ),
    )(
        weights.reshape(2, features, width),
        saved.reshape(pieces, rows, features),
        cotangent.reshape(pieces, rows, features),
    )
    normed_all = normed_all.reshape(-1, cut)
    wide_all = wide_all.reshape(-1, cut)
    narrow_all = narrow_all.reshape(-1, width)
    down_part = jnp.einsum("td,tk->dk", normed_all, narrow_all[:, :rank], preferred_element_type=f32)
    up_part = jnp.einsum("td,tk->dk", wide_all, narrow_all[:, rank:], preferred_element_type=f32)
    gradient = jnp.concatenate([down_part, up_part], axis=1)
    new_master, new_first, new_second = adamw(master[0], moment1[0], moment2[0], gradient)
    return (new_master[None], new_first[None], new_second[None])


def solution(mesh):
    return jax.shard_map(
        shards,
        mesh=mesh,
        in_specs=(
            P("pipe", None, None, None),
            P("pipe", "dp", None),
            P("pipe", "dp", None),
            P("pipe", "dp", None),
            P("pipe", None, None, "dp", None),
            P(None, None, "dp", None),
        ),
        out_specs=(P("pipe", "dp", None), P("pipe", "dp", None), P("pipe", "dp", None)),
        check_vma=False,
    )
```

```python
import functools

import jax
import jax.numpy as jnp
from jax import lax
from jax.experimental import pallas as pl
from jax.experimental.pallas import tpu as pltpu
from jax.sharding import PartitionSpec as P

norm_epsilon = 1e-06
first_decay = 0.9
second_decay = 0.95
adam_epsilon = 1e-08
learn_rate = 0.00022
weight_decay = 0.1
step_count = 100.0


def adamw(master, moment1, moment2, gradient):
    first_new = first_decay * moment1.astype(jnp.float32) + (1.0 - first_decay) * gradient
    second_new = (
        second_decay * moment2.astype(jnp.float32) + (1.0 - second_decay) * gradient * gradient
    )
    first_hat = first_new / (1.0 - first_decay**step_count)
    second_hat = second_new / (1.0 - second_decay**step_count)
    updated = master - learn_rate * (
        first_hat / (jnp.sqrt(second_hat) + adam_epsilon) + weight_decay * master
    )
    return (updated, first_new.astype(jnp.bfloat16), second_new.astype(jnp.bfloat16))


def chain_kernel(
    n_dp, sections, weights_ref, saved_ref, cot_ref,
    normed_all, wide_all, narrow_all,
    w, here, arrived, outgoing, swapped, normed_cut, wide_cut, latents, scales,
    w_sem, here_sem, cot_sem, ex_send, ex_recv, chain_send, chain_recv, swap_send, swap_recv,
):
    me = lax.axis_index("dp")
    position = lax.axis_index("pipe")
    pieces, rows, features = saved_ref.shape
    half = pieces // 2
    rank = w.shape[1] // 2
    cut = features // n_dp
    chunks = chain_send.shape[1]
    chunk = features // chunks
    columns = [pl.ds(c * chunk, chunk) for c in range(chunks)]
    partner = sections - 1 - position
    below = lax.rem(position + sections - 1, sections)
    above = lax.rem(position + 1, sections)

    w_copy = pltpu.make_async_copy(weights_ref.at[0], w, w_sem)
    w_copy.start()
    here_copy = pltpu.make_async_copy(saved_ref.at[pl.ds(0, half)], here, here_sem)
    here_copy.start()
    cot_copy = pltpu.make_async_copy(cot_ref, arrived, cot_sem)

    @pl.when(position == sections - 1)
    def _():
        cot_copy.start()

    barrier = pltpu.get_barrier_semaphore()

    def greet(device):
        pl.semaphore_signal(
            barrier, inc=1, device_id=device, device_id_type=pl.DeviceIdType.MESH
        )

    for apart in range(1, n_dp):
        greet({"dp": lax.rem(me + apart, n_dp)})
    for device in (partner, below, above):
        greet({"pipe": device})
    pl.semaphore_wait(barrier, n_dp + 2)

    def remote(source, target, send, receive, device):
        return pltpu.make_async_remote_copy(
            src_ref=source, dst_ref=target, send_sem=send, recv_sem=receive,
            device_id=device, device_id_type=pl.DeviceIdType.MESH,
        )

    def swap_copy(h, c):
        return remote(
            saved_ref.at[half + h, :, columns[c]], swapped.at[h, :, columns[c]],
            swap_send.at[h, c], swap_recv.at[h, c], {"pipe": partner},
        )

    def swap_each(act):
        for h in range(half):
            for c in range(chunks):
                act(swap_copy(h, c))

    def chain_copy(k, c):
        return remote(
            outgoing.at[k, :, columns[c]], arrived.at[k, :, columns[c]],
            chain_send.at[k, c], chain_recv.at[k, c], {"pipe": below},
        )

    def exchange(kind, apart, k):
        peer = lax.rem(me + apart, n_dp)
        target = (normed_all, wide_all, narrow_all)[kind]
        source = (
            normed_cut.at[peer, k], wide_cut.at[peer, k], narrow_all.at[0, k]
        )[kind]
        return remote(
            source, target.at[apart, k], ex_send.at[kind, apart, k],
            ex_recv.at[kind, apart, k], {"dp": peer},
        )

    swap_each(lambda copy: copy.start())

    here_copy.wait()
    w_copy.wait()

    def prepare(k):
        if k < half:
            x = here[k]
        else:
            for c in range(chunks):
                swap_copy(k - half, c).wait_recv()
            x = swapped[k - half]
        values = x.astype(jnp.float32)
        row_scale = lax.rsqrt(jnp.mean(values * values, axis=-1, keepdims=True) + norm_epsilon)
        normed = (values * row_scale).astype(jnp.bfloat16)
        latent = jnp.dot(normed, w[:, :rank], preferred_element_type=jnp.float32)
        latents[k] = latent
        scales[k] = jnp.broadcast_to(row_scale, scales.shape[1:])
        latent_scale = lax.rsqrt(jnp.mean(latent * latent, axis=-1, keepdims=True) + norm_epsilon)
        narrow_all[0, k, :, rank:] = (latent * latent_scale).astype(jnp.bfloat16)
        for owner in range(n_dp):
            normed_cut[owner, k] = normed[:, owner * cut : (owner + 1) * cut]
        for apart in range(1, n_dp):
            exchange(0, apart, k).start()
        normed_all[0, k] = normed_cut[me, k]

    def advance(k):
        @pl.when(position == sections - 1)
        def _():
            if k == 0:
                cot_copy.wait()

        latent = latents[k]
        row_scale = scales[k][:, :1]
        latent_scale = lax.rsqrt(jnp.mean(latent * latent, axis=-1, keepdims=True) + norm_epsilon)
        grad_act = jnp.zeros((rows, rank), jnp.float32)
        for c in range(chunks):

            @pl.when(position < sections - 1)
            def _():
                chain_copy(k, c).wait_recv()

            grad_act += jnp.dot(
                arrived[k, :, columns[c]], w[columns[c], rank:],
                preferred_element_type=jnp.float32,
            )
        grad_latent = latent_scale * grad_act - latent * latent_scale**3 * jnp.mean(
            latent * grad_act, axis=-1, keepdims=True
        )
        grad_latent = grad_latent.astype(jnp.bfloat16)
        narrow_all[0, k, :, :rank] = grad_latent

        @pl.when(position > 0)
        def _():
            along = jnp.sum(latent * grad_latent.astype(jnp.float32), axis=-1, keepdims=True)
            along = along * (row_scale * row_scale / features)
            x_ref = here.at[k] if k < half else swapped.at[k - half]
            for c in range(chunks):
                grad_normed = lax.dot_general(
                    grad_latent, w[columns[c], :rank], (((1,), (1,)), ((), ())),
                    preferred_element_type=jnp.float32,
                )
                outgoing[k, :, columns[c]] = (
                    arrived[k, :, columns[c]].astype(jnp.float32)
                    + row_scale * grad_normed
                    - x_ref[:, columns[c]].astype(jnp.float32) * along
                ).astype(jnp.bfloat16)
                chain_copy(k, c).start()

        for owner in range(n_dp):
            wide_cut[owner, k] = arrived[k, :, owner * cut : (owner + 1) * cut]
        for apart in range(1, n_dp):
            exchange(1, apart, k).start()
            exchange(2, apart, k).start()
        wide_all[0, k] = wide_cut[me, k]

    prepare(0)

    for k in range(pieces):
        advance(k)
        if k + 1 < pieces:
            prepare(k + 1)

    swap_each(lambda copy: copy.wait_send())

    @pl.when(position > 0)
    def _():
        for k in range(pieces):
            for c in range(chunks):
                chain_copy(k, c).wait_send()

    for kind in range(3):
        for apart in range(1, n_dp):
            for k in range(pieces):
                exchange(kind, apart, k).wait()


def shards(weights, master, moment1, moment2, saved, cotangent):
    n_dp = lax.axis_size("dp")
    sections = lax.axis_size("pipe")
    micro, batch_rows, features = saved.shape[2:]
    width = weights.shape[3]
    rank = width // 2
    pieces = 2 * micro
    rows = 2 * micro * batch_rows // pieces
    cut = features // n_dp
    chunks = 3 if features % (3 * 128) == 0 else 1
    bf16, f32 = jnp.bfloat16, jnp.float32
    vmem = pl.BlockSpec(memory_space=pltpu.VMEM)
    flops = 2 * pieces * rows * features * rank * 3
    normed_all, wide_all, narrow_all = pl.pallas_call(
        functools.partial(chain_kernel, n_dp, sections),
        out_shape=[
            jax.ShapeDtypeStruct((n_dp, pieces, rows, cut), bf16),
            jax.ShapeDtypeStruct((n_dp, pieces, rows, cut), bf16),
            jax.ShapeDtypeStruct((n_dp, pieces, rows, width), bf16),
        ],
        in_specs=[pl.BlockSpec(memory_space=pl.ANY)] * 3,
        out_specs=[vmem, vmem, vmem],
        scratch_shapes=[
            pltpu.VMEM((features, width), bf16),
            pltpu.VMEM((pieces // 2, rows, features), bf16),
            pltpu.VMEM((pieces, rows, features), bf16),
            pltpu.VMEM((pieces, rows, features), bf16),
            pltpu.VMEM((pieces // 2, rows, features), bf16),
            pltpu.VMEM((n_dp, pieces, rows, cut), bf16),
            pltpu.VMEM((n_dp, pieces, rows, cut), bf16),
            pltpu.VMEM((pieces, rows, rank), f32),
            pltpu.VMEM((pieces, rows, 128), f32),
            pltpu.SemaphoreType.DMA,
            pltpu.SemaphoreType.DMA,
            pltpu.SemaphoreType.DMA,
            pltpu.SemaphoreType.DMA((3, n_dp, pieces)),
            pltpu.SemaphoreType.DMA((3, n_dp, pieces)),
            pltpu.SemaphoreType.DMA((pieces, chunks)),
            pltpu.SemaphoreType.DMA((pieces, chunks)),
            pltpu.SemaphoreType.DMA((pieces // 2, chunks)),
            pltpu.SemaphoreType.DMA((pieces // 2, chunks)),
        ],
        compiler_params=pltpu.CompilerParams(
            collective_id=0, has_side_effects=True, vmem_limit_bytes=44 * 2**20
        ),
        cost_estimate=pl.CostEstimate(
            flops=flops, bytes_accessed=features * width * 2, transcendentals=0
        ),
    )(
        weights.reshape(2, features, width),
        saved.reshape(pieces, rows, features),
        cotangent.reshape(pieces, rows, features),
    )
    normed_all = normed_all.reshape(-1, cut)
    wide_all = wide_all.reshape(-1, cut)
    narrow_all = narrow_all.reshape(-1, width)
    down_part = jnp.einsum("td,tk->dk", normed_all, narrow_all[:, :rank], preferred_element_type=f32)
    up_part = jnp.einsum("td,tk->dk", wide_all, narrow_all[:, rank:], preferred_element_type=f32)
    gradient = jnp.concatenate([down_part, up_part], axis=1)
    new_master, new_first, new_second = adamw(master[0], moment1[0], moment2[0], gradient)
    return (new_master[None], new_first[None], new_second[None])


def solution(mesh):
    return jax.shard_map(
        shards,
        mesh=mesh,
        in_specs=(
            P("pipe", None, None, None),
            P("pipe", "dp", None),
            P("pipe", "dp", None),
            P("pipe", "dp", None),
            P("pipe", None, None, "dp", None),
            P(None, None, "dp", None),
        ),
        out_specs=(P("pipe", "dp", None), P("pipe", "dp", None), P("pipe", "dp", None)),
        check_vma=False,
    )
```
